128 devices in a mesh: frame: 16 (over z_lo, x, core), head: 8 (over z_hi, y).
Axes of the slice: x: 4, y: 4, z: 4 (z_hi: 2, z_lo: 2; z = z_hi * 2 + z_lo), core: 2. Of those that a mesh axis runs over, the one named last changes fastest.
Arguments:
- hidden_in: bfloat16 [10240, 5120], P('frame', 'head'), may hold values from -6 to 6
- queries: bfloat16 [10240, 5120], P('frame', 'head'), may hold values from -90 to 90
- keys: bfloat16 [10240, 5120], P('frame', 'head'), may hold values from -5 to 5
- values: bfloat16 [10240, 5120], P('frame', 'head'), may hold values from -6 to 6
- radial_mask: int32 [16, 6, 5, 5], P('frame'), may hold values from 0 to 1, as said below
- out_weight: bfloat16 [5120, 5120], P('head'), may hold values from -0.078125 to 0.078125
- gate_table: float32 [50, 5120], P(None, 'head'), may hold values from -4 to 4
- timestep: int32 [1], replicated, may hold values from 0 to 49
Outputs:
- layer_out: bfloat16 [10240, 5120], P('frame', 'head')
The draws below stay inside these ranges and needn't reach their ends.
Inputs may be any that keep to these rules, and one draw needn't show every extreme that they name: `radial_mask`: an entry whose key frame lies outside the video is 0.
All inputs are finite; a program needn't handle non-finite values.
Results may differ from the reference program's by a relative error of at most 0.0055.
Values may be sent and summed in bfloat16 or wider, within the bound.
A program may use at most 192 MiB of HBM per device.

```python
import jax
import jax.numpy as jnp
from jax import lax

HEAD_DIM = 128
HEADS = 40
D = 5120
TOK_FRAME = 640
BLK = 128
NB = 5
FRAMES = 16
TOKENS = 10240
STEPS = 50
N_HEAD = 8


def paired_draw(key):
    width = HEADS * HEAD_DIM
    key_base = jnp.clip(jax.random.normal(jax.random.fold_in(key, 11), (TOKENS, width), jnp.float32), -4.0, 4.0)
    query_base = jnp.clip(jax.random.normal(jax.random.fold_in(key, 12), (TOKENS, width), jnp.float32), -4.0, 4.0)
    return (query_base, key_base)


def draw_queries(key, part):
    drawn = paired_draw(key)
    return drawn[0].astype(jnp.bfloat16)


def draw_keys(key, part):
    drawn = paired_draw(key)
    return drawn[1].astype(jnp.bfloat16)


def draw_radial_mask(key, part):
    key = jax.random.fold_in(key, 3)
    throws = jax.random.randint(key, (FRAMES, 6, NB, NB), 0, 8)
    levels = jnp.array([1, 2, 4, 4, 2, 1], jnp.int32)
    offsets = jnp.array([-8, -4, -2, 2, 4, 8], jnp.int32)
    source = jnp.arange(FRAMES, dtype=jnp.int32)[:, None] + offsets[None, :]
    inside = jnp.logical_and(source >= 0, source < FRAMES)
    chosen = jnp.logical_and(throws < levels[None, :, None, None], inside[:, :, None, None])
    return chosen.astype(jnp.int32)


def shard_levels(stream_key, dims, cuts, low, top_value):
    level, own = 1.0, jax.random.fold_in(stream_key, 6)
    for dim, blocks in cuts:
        draws = jnp.exp(jax.random.uniform(jax.random.fold_in(own, dim), (blocks,), jnp.float32, low / len(cuts), top_value / len(cuts)))
        level = level * jnp.repeat(draws, dims[dim] // blocks).reshape([-1 if axis == dim else 1 for axis in range(len(dims))])
    return level


def noise(rng, dims, deviation, limit, cuts=(), kind=jnp.bfloat16):
    result = jax.random.normal(rng, dims, jnp.float32) * deviation
    if len(cuts) > 0:
        result = shard_levels(rng, dims, cuts, -0.22, 0.18) * result
    return jnp.clip(result, min=-limit, max=limit).astype(kind)


def setup_inputs(seed: int = 0) -> dict:
    streams_of = jax.random.split(jax.random.key(seed), 9)
    return {
        "hidden_in": noise(streams_of[0], (TOKENS, D), 1.0, 6.0, ((0, 16), (1, 8))),
        "queries": draw_queries(jax.random.fold_in(streams_of[8], 71), 0),
        "keys": draw_keys(jax.random.fold_in(streams_of[8], 71), 0),
        "values": noise(streams_of[3], (TOKENS, D), 1.0, 6.0, ((0, 16), (1, 8))),
        "radial_mask": draw_radial_mask(jax.random.fold_in(streams_of[8], 71), 0),
        "out_weight": noise(streams_of[5], (D, D), D ** -0.5, 0.078125, ((0, 8),)),
        "gate_table": noise(streams_of[6], (STEPS, D), 1.0, 4.0, ((1, 8),), jnp.float32),
        "timestep": jax.random.randint(streams_of[7], (1,), 0, STEPS).astype(jnp.int32),
    }


far_offsets = (-8, -4, -2, 2, 4, 8)
all_offsets = (-8, -4, -2, -1, 0, 1, 2, 4, 8)
neg_large = -1.0e30


def expand_blocks(blocks):
    return jnp.repeat(jnp.repeat(blocks, BLK, axis=0), BLK, axis=1) > 0


def frame_attention(frame_index, query_all, key_all, value_all, radial_mask):
    key_parts = []
    value_parts = []
    mask_parts = []
    mask_rows = lax.dynamic_index_in_dim(radial_mask, frame_index, 0, keepdims=False)
    for offset in all_offsets:
        source = frame_index + offset
        inside = jnp.logical_and(source >= 0, source < FRAMES)
        clipped = jnp.clip(source, 0, FRAMES - 1).astype(jnp.int32)
        key_parts.append(lax.dynamic_index_in_dim(key_all, clipped, 0, keepdims=False))
        value_parts.append(lax.dynamic_index_in_dim(value_all, clipped, 0, keepdims=False))
        if offset in far_offsets:
            blocks = mask_rows[far_offsets.index(offset)]
        else:
            blocks = jnp.ones((NB, NB), jnp.int32) * inside.astype(jnp.int32)
        mask_parts.append(expand_blocks(blocks))
    key_joined = jnp.concatenate(key_parts, axis=0)
    value_joined = jnp.concatenate(value_parts, axis=0)
    allowed = jnp.concatenate(mask_parts, axis=1)
    query_frame = lax.dynamic_index_in_dim(query_all, frame_index, 0, keepdims=False)
    scale = HEAD_DIM ** -0.5

    def one_head(operands):
        query_head, key_head, value_head = operands
        scores = jnp.dot(query_head, key_head.T, preferred_element_type=jnp.float32) * scale
        scores = jnp.where(allowed, scores, neg_large)
        row_max = jnp.max(scores, axis=-1, keepdims=True)
        weights = jnp.where(allowed, jnp.exp(scores - row_max), 0.0)
        row_total = jnp.sum(weights, axis=-1)
        mixed = jnp.dot(weights.astype(jnp.bfloat16), value_head, preferred_element_type=jnp.float32)
        return (mixed / row_total[:, None]).astype(jnp.bfloat16)

    return lax.map(one_head, (query_frame.transpose(1, 0, 2), key_joined.transpose(1, 0, 2), value_joined.transpose(1, 0, 2)))


def reference(hidden_in, queries, keys, values, radial_mask, out_weight, gate_table, timestep):
    query_all = queries.reshape(FRAMES, TOK_FRAME, HEADS, HEAD_DIM)
    key_all = keys.reshape(FRAMES, TOK_FRAME, HEADS, HEAD_DIM)
    value_all = values.reshape(FRAMES, TOK_FRAME, HEADS, HEAD_DIM)

    def per_frame(frame_index):
        return frame_attention(frame_index, query_all, key_all, value_all, radial_mask)

    attended = lax.map(per_frame, jnp.arange(FRAMES, dtype=jnp.int32))
    attended = attended.transpose(0, 2, 1, 3).reshape(TOKENS, HEADS * HEAD_DIM)
    group_width = (HEADS * HEAD_DIM) // N_HEAD
    projected = jnp.zeros((TOKENS, HEADS * HEAD_DIM), jnp.float32)
    for group_index in range(N_HEAD):
        columns = attended[:, group_index * group_width:(group_index + 1) * group_width]
        rows_part = out_weight[group_index * group_width:(group_index + 1) * group_width]
        term = jnp.dot(columns, rows_part, preferred_element_type=jnp.float32).astype(jnp.bfloat16)
        term = lax.optimization_barrier(term)
        projected = projected + term.astype(jnp.float32)
    gate = gate_table[timestep[0]].astype(jnp.float32)
    return (hidden_in.astype(jnp.float32) + gate[None, :] * projected).astype(jnp.bfloat16)
```

```python
import functools

import jax
import jax.numpy as jnp
from jax import lax
from jax.experimental import pallas as pl
from jax.experimental.pallas import tpu as pltpu
from jax.sharding import PartitionSpec as P

MESH = pl.DeviceIdType.MESH
HEAD_DIM = 128
BLK = 128
ROWS = 640
HEADS_LOCAL = 5
GROUPS = 8
SLOTS = 9
OWN, SIB, LEFT, RIGHT, FAR8, FWD, LEFT2, RIGHT2, RELAY = range(9)
SCALE2 = 1.4426950408889634 * HEAD_DIM ** -0.5
NEG = -1e30
HALF = ROWS // 2


def both(*conds):
    out = conds[0]
    for c in conds[1:]:
        out = jnp.logical_and(out, c)
    return out


def kernel(ts_ref, mask_ref, gate_ref, hid_hbm, q_hbm, k_hbm, v_hbm, w_hbm, out_ref,
           kv, qs, att, wcol, hid, bias, m_s, l_s, acc, proj,
           loc, kv_send, kv_recv, at_send, at_recv, w_send, w_recv, ws_send, ws_recv):
    f = lax.axis_index("frame")
    g = lax.axis_index("head")
    core = lax.rem(f, 2)
    sib = f + 1 - 2 * core
    f8 = lax.rem(f + 8, 16)
    zh = g // 4
    y = lax.rem(g, 4)
    other = 1 - zh

    def same(j):
        return zh * 4 + lax.rem(y + j, 4)

    def cross(j):
        return other * 4 + lax.rem(y + j, 4)

    is_a = f < 2
    is_b = both(f >= 6, f < 8)
    is_c = both(f >= 8, f < 10)
    is_d = f >= 14
    not_b = jnp.logical_or(f < 6, f >= 8)
    not_c = jnp.logical_or(f < 8, f >= 10)
    always = f >= 0
    inner = both(f >= 2, f < 14)
    odd = core == 1
    even = core == 0

    local = []
    for h in range(HEADS_LOCAL):
        cols = pl.ds(h * HEAD_DIM, HEAD_DIM)
        local.append([
            pltpu.make_async_copy(k_hbm.at[:, cols], kv.at[OWN, h, 0], loc.at[3 * h]),
            pltpu.make_async_copy(v_hbm.at[:, cols], kv.at[OWN, h, 1], loc.at[3 * h + 1]),
            pltpu.make_async_copy(q_hbm.at[:, cols], qs.at[h], loc.at[3 * h + 2]),
        ])
    for copies in local:
        for c in copies:
            c.start()
    own_cols = pl.ds(pl.multiple_of(g * ROWS, 128), ROWS)
    w_local = pltpu.make_async_copy(w_hbm.at[:, own_cols], wcol.at[g], loc.at[15])
    hid_local = pltpu.make_async_copy(hid_hbm, hid, loc.at[16])

    barrier = pltpu.get_barrier_semaphore()
    peers = [
        (always, (sib, g)), (always, (f8, g)),
        (both(f < 14, not_b), (f + 2, g)), (both(f >= 2, not_c), (f - 2, g)),
        (jnp.logical_or(is_a, is_c), (f + 6, g)), (jnp.logical_or(is_b, is_d), (f - 6, g)),
        (always, (f, cross(0))),
    ]
    peers += [(always, (f, same(j))) for j in (1, 2, 3)]
    peers += [(always, (f8, cross(j))) for j in range(4)]
    count = 0
    for cond, dev in peers:
        if cond is always:
            pl.semaphore_signal(barrier, inc=1, device_id=dev, device_id_type=MESH)
            count = count + 1
        else:
            @pl.when(cond)
            def _(dev=dev):
                pl.semaphore_signal(barrier, inc=1, device_id=dev, device_id_type=MESH)
            count = count + jnp.where(cond, 1, 0)
    pl.semaphore_wait(barrier, count)

    edges = [
        (0, always, OWN, SIB, sib),
        (1, both(f < 14, not_b), OWN, LEFT, f + 2),
        (2, both(f >= 2, not_c), OWN, RIGHT, f - 2),
        (3, always, OWN, FAR8, f8),
        (4, both(inner, not_b), LEFT, LEFT2, f + 2),
        (4, is_b, LEFT, RELAY, f - 6),
        (5, both(inner, not_c), RIGHT, RIGHT2, f - 2),
        (5, is_c, RIGHT, RELAY, f + 6),
        (6, both(odd, f >= 2), LEFT, FWD, f - 1),
        (6, both(even, f < 14), RIGHT, FWD, f + 1),
        (7, is_d, FAR8, LEFT, f - 6),
        (7, is_a, FAR8, RIGHT, f + 6),
        (8, is_a, RELAY, LEFT2, f + 8),
        (8, is_d, RELAY, RIGHT2, f - 8),
    ]

    def kv_copy(h, edge):
        kind, _, src, dst, to = edge
        return pltpu.make_async_remote_copy(
            src_ref=kv.at[src, h], dst_ref=kv.at[dst, h],
            send_sem=kv_send.at[kind, h], recv_sem=kv_recv.at[dst, h],
            device_id=(to, g), device_id_type=MESH)

    def kv_start(h, *kinds):
        for edge in edges:
            if edge[0] in kinds:
                if edge[1] is always:
                    kv_copy(h, edge).start()
                else:
                    @pl.when(edge[1])
                    def _(edge=edge):
                        kv_copy(h, edge).start()

    has = {
        SIB: always, FAR8: always, LEFT: f >= 2, RIGHT: f < 14, LEFT2: f >= 4, RIGHT2: f < 12,
        FWD: jnp.logical_or(both(even, f >= 2), both(odd, f < 14)),
        RELAY: jnp.logical_or(is_a, is_d),
    }

    def kv_wait(h, slot):
        def wait():
            pltpu.make_async_remote_copy(
                src_ref=kv.at[slot, h], dst_ref=kv.at[slot, h],
                send_sem=kv_send.at[0, h], recv_sem=kv_recv.at[slot, h],
                device_id=(sib, g), device_id_type=MESH).wait_recv()
        if has[slot] is always:
            wait()
        else:
            pl.when(has[slot])(wait)

    half = pl.ds(pl.multiple_of(core * HALF, 16), HALF)
    w_peers = [(f, same(j)) for j in (1, 2, 3)] + [(f8, cross(j)) for j in range(4)]

    def w_copy(i):
        frame, group = w_peers[i]
        cols = pl.ds(pl.multiple_of(group * ROWS, 128), ROWS)
        return pltpu.make_async_remote_copy(
            src_ref=w_hbm.at[half, cols], dst_ref=wcol.at[g, half],
            send_sem=w_send.at[i], recv_sem=w_recv.at[g],
            device_id=(frame, group), device_id_type=MESH)

    def w_wait(i):
        group = w_peers[i][1]
        pltpu.make_async_remote_copy(
            src_ref=wcol.at[group, half], dst_ref=wcol.at[group, half],
            send_sem=w_send.at[i], recv_sem=w_recv.at[group],
            device_id=(sib, g), device_id_type=MESH).wait_recv()

    def w_forward(i):
        group = w_peers[i][1]
        return pltpu.make_async_remote_copy(
            src_ref=wcol.at[group, half], dst_ref=wcol.at[group, half],
            send_sem=ws_send.at[i], recv_sem=ws_recv.at[group],
            device_id=(sib, g), device_id_type=MESH)

    def ws_wait(i):
        group = w_peers[i][1]
        theirs = pl.ds(pl.multiple_of((1 - core) * HALF, 16), HALF)
        pltpu.make_async_remote_copy(
            src_ref=wcol.at[group, theirs], dst_ref=wcol.at[group, theirs],
            send_sem=ws_send.at[i], recv_sem=ws_recv.at[group],
            device_id=(sib, g), device_id_type=MESH).wait_recv()

    gathers = [
        (0, g, cross(0)), (1, g, same(1)), (2, g, same(3)),
        (3, cross(0), same(1)), (4, cross(0), same(3)),
        (5, same(3), same(1)), (6, cross(1), same(3)),
    ]

    def at_copy(h, kind):
        _, group, to = gathers[kind]
        return pltpu.make_async_remote_copy(
            src_ref=att.at[group, h], dst_ref=att.at[group, h],
            send_sem=at_send.at[kind, h], recv_sem=at_recv.at[group, h],
            device_id=(f, to), device_id_type=MESH)

    def at_wait(h, group):
        pltpu.make_async_remote_copy(
            src_ref=att.at[group, h], dst_ref=att.at[group, h],
            send_sem=at_send.at[0, h], recv_sem=at_recv.at[group, h],
            device_id=(sib, g), device_id_type=MESH).wait_recv()

    def relay_attended(h):
        at_wait(h, cross(0))
        at_copy(h, 3).start()
        at_copy(h, 4).start()
        at_wait(h, same(3))
        at_copy(h, 5).start()
        at_wait(h, cross(1))
        at_copy(h, 6).start()

    def project(h):
        at_wait(h, same(1))
        at_wait(h, same(2))
        at_wait(h, cross(2))
        at_wait(h, cross(3))
        rows = pl.ds(pl.multiple_of(h * HEAD_DIM, 128), HEAD_DIM)
        lhs = jnp.concatenate([att[i, h] for i in range(GROUPS)], axis=1)
        rhs = jnp.concatenate([wcol[i, rows, :] for i in range(GROUPS)], axis=0)
        proj[...] += jnp.dot(lhs, rhs, preferred_element_type=jnp.float32)

    far_row = {LEFT: 0, RIGHT: 1, FAR8: 2, LEFT2: 3, RIGHT2: 4}

    def attend(h, slot):
        def run():
            s_all = lax.dot_general(
                qs[h], kv[slot, h, 0], (((1,), (1,)), ((), ())),
                preferred_element_type=jnp.float32)
            weights = []
            for b in range(ROWS // BLK):
                rows = slice(b * BLK, (b + 1) * BLK)
                s = s_all[rows]
                if slot in far_row:
                    s = s + bias[far_row[slot], b:b + 1, :]
                top = functools.reduce(
                    jnp.maximum, [s[:, i * 128:(i + 1) * 128] for i in range(5)])
                old = m_s[rows, :]
                new = jnp.maximum(old, jnp.max(top, axis=1, keepdims=True))
                factor = jnp.exp2((old - new) * SCALE2)
                parts = [jnp.exp2((s[:, i * 128:(i + 1) * 128] - new) * SCALE2) for i in range(5)]
                m_s[rows, :] = new
                l_s[rows, :] = l_s[rows, :] * factor + functools.reduce(jnp.add, parts)
                acc[rows, :] = acc[rows, :] * factor
                weights.append(jnp.concatenate([p.astype(jnp.bfloat16) for p in parts], axis=1))
            acc[...] += jnp.dot(
                jnp.concatenate(weights, axis=0), kv[slot, h, 1],
                preferred_element_type=jnp.float32)
        cond = always if slot == OWN else has[slot]
        if cond is always:
            run()
        else:
            pl.when(cond)(run)

    for h in range(2):
        for c in local[h]:
            c.wait()
        kv_start(h, 1, 2, 3, 0)
    w_local.start()
    hid_local.start()
    for i in range(7):
        w_copy(i).start()
    for h in range(2, HEADS_LOCAL):
        for c in local[h]:
            c.wait()

    far8_row = 5 - 5 * (f // 8)
    for slot, source in ((LEFT, 2), (RIGHT, 3), (FAR8, far8_row), (LEFT2, 1), (RIGHT2, 4)):
        for a in range(5):
            for b in range(5):
                value = (mask_ref[0, source, a, b].astype(jnp.float32) - 1.0) * (-NEG)
                bias[far_row[slot], a:a + 1, b * BLK:(b + 1) * BLK] = jnp.full((1, BLK), value, jnp.float32)
    proj[...] = jnp.zeros_like(proj)
    w_local.wait()
    hid_local.wait()

    def phase(h, _):
        @pl.when(both(h >= 1, h < HEADS_LOCAL - 1))
        def _():
            kv_start(h + 1, 1, 2, 3, 0)

        m_s[...] = jnp.full_like(m_s, NEG)
        l_s[...] = jnp.zeros_like(l_s)
        acc[...] = jnp.zeros_like(acc)
        attend(h, OWN)
        kv_wait(h, SIB)
        attend(h, SIB)
        kv_wait(h, FAR8)
        kv_start(h, 7)
        kv_wait(h, LEFT)
        kv_wait(h, RIGHT)
        kv_start(h, 4, 5, 6)
        attend(h, FAR8)
        attend(h, LEFT)
        attend(h, RIGHT)
        kv_wait(h, RELAY)
        kv_start(h, 8)

        @pl.when(h >= 1)
        def _():
            relay_attended(h - 1)

        @pl.when(h == 1)
        def _():
            for i in range(7):
                w_wait(i)
                w_forward(i).start()

        kv_wait(h, FWD)
        attend(h, FWD)

        @pl.when(h == 2)
        def _():
            for i in range(7):
                ws_wait(i)

        @pl.when(h >= 2)
        def _():
            project(h - 2)

        kv_wait(h, LEFT2)
        attend(h, LEFT2)
        kv_wait(h, RIGHT2)
        attend(h, RIGHT2)
        total = jnp.sum(l_s[...], axis=1, keepdims=True)
        att[g, h] = (acc[...] / total).astype(jnp.bfloat16)
        at_copy(h, 0).start()
        at_copy(h, 1).start()
        at_copy(h, 2).start()
        return 0

    lax.fori_loop(0, HEADS_LOCAL, phase, 0)
    relay_attended(HEADS_LOCAL - 1)
    project(HEADS_LOCAL - 2)
    project(HEADS_LOCAL - 1)
    gate = gate_ref[pl.ds(ts_ref[0], 1), :]
    out_ref[...] = (hid[...].astype(jnp.float32) + gate * proj[...]).astype(out_ref.dtype)

    def drain(h, _):
        for edge in edges:
            if edge[1] is always:
                kv_copy(h, edge).wait_send()
            else:
                @pl.when(edge[1])
                def _(edge=edge):
                    kv_copy(h, edge).wait_send()
        for kind in range(len(gathers)):
            at_copy(h, kind).wait_send()
        return 0

    lax.fori_loop(0, HEADS_LOCAL, drain, 0)
    for i in range(7):
        w_copy(i).wait_send()
        w_forward(i).wait_send()


def body(hidden_in, queries, keys, values, radial_mask, out_weight, gate_table, timestep):
    any_spec = pl.BlockSpec(memory_space=pl.ANY)
    dma = pltpu.SemaphoreType.DMA
    return pl.pallas_call(
        kernel,
        out_shape=jax.ShapeDtypeStruct((ROWS, ROWS), jnp.bfloat16),
        in_specs=[
            pl.BlockSpec(memory_space=pltpu.SMEM),
            pl.BlockSpec(memory_space=pltpu.SMEM),
            pl.BlockSpec(memory_space=pltpu.VMEM),
            any_spec, any_spec, any_spec, any_spec, any_spec,
        ],
        out_specs=pl.BlockSpec(memory_space=pltpu.VMEM),
        scratch_shapes=[
            pltpu.VMEM((SLOTS, HEADS_LOCAL, 2, ROWS, HEAD_DIM), jnp.bfloat16),
            pltpu.VMEM((HEADS_LOCAL, ROWS, HEAD_DIM), jnp.bfloat16),
            pltpu.VMEM((GROUPS, HEADS_LOCAL, ROWS, HEAD_DIM), jnp.bfloat16),
            pltpu.VMEM((GROUPS, ROWS, ROWS), jnp.bfloat16),
            pltpu.VMEM((ROWS, ROWS), jnp.bfloat16),
            pltpu.VMEM((5, 5, ROWS), jnp.float32),
            pltpu.VMEM((ROWS, HEAD_DIM), jnp.float32),
            pltpu.VMEM((ROWS, HEAD_DIM), jnp.float32),
            pltpu.VMEM((ROWS, HEAD_DIM), jnp.float32),
            pltpu.VMEM((ROWS, ROWS), jnp.float32),
            dma((17,)),
            dma((9, HEADS_LOCAL)), dma((SLOTS, HEADS_LOCAL)),
            dma((7, HEADS_LOCAL)), dma((GROUPS, HEADS_LOCAL)),
            dma((7,)), dma((GROUPS,)), dma((7,)), dma((GROUPS,)),
        ],
        compiler_params=pltpu.CompilerParams(
            collective_id=0, has_side_effects=True, vmem_limit_bytes=60 * 1024 * 1024),
        cost_estimate=pl.CostEstimate(
            flops=14_000_000_000, bytes_accessed=12_000_000, transcendentals=16_000_000),
    )(timestep, radial_mask, gate_table, hidden_in, queries, keys, values, out_weight)


def solution(mesh):
    in_specs = (
        P("frame", "head"), P("frame", "head"), P("frame", "head"), P("frame", "head"),
        P("frame", None, None, None), P("head", None), P(None, "head"), P(),
    )
    return jax.shard_map(
        body, mesh=mesh, in_specs=in_specs, out_specs=P("frame", "head"), check_vma=False)
```

```python
import functools

import jax
import jax.numpy as jnp
from jax import lax
from jax.experimental import pallas as pl
from jax.experimental.pallas import tpu as pltpu
from jax.sharding import PartitionSpec as P

MESH = pl.DeviceIdType.MESH
HEAD_DIM = 128
BLK = 128
ROWS = 640
HEADS_LOCAL = 5
GROUPS = 8
SLOTS = 9
OWN, SIB, LEFT, RIGHT, FAR8, FWD, LEFT2, RIGHT2, RELAY = range(9)
SCALE2 = 1.4426950408889634 * HEAD_DIM ** -0.5
NEG = -1e30
HALF = ROWS // 2
AHEAD = 2


def both(*conds):
    out = conds[0]
    for c in conds[1:]:
        out = jnp.logical_and(out, c)
    return out


def kernel(ts_ref, mask_hbm, gate_hbm, hid_hbm, q_hbm, k_hbm, v_hbm, w_hbm, out_ref,
           kv, qs, att, wcol, hid, mask_s, gate_s, bias, m_s, l_s, acc, proj,
           loc, kv_send, kv_recv, at_send, at_recv, w_send, w_recv, ws_send, ws_recv):
    f = lax.axis_index("frame")
    g = lax.axis_index("head")
    core = lax.rem(f, 2)
    sib = f + 1 - 2 * core
    f8 = lax.rem(f + 8, 16)
    zh = g // 4
    y = lax.rem(g, 4)
    other = 1 - zh

    def same(j):
        return zh * 4 + lax.rem(y + j, 4)

    def cross(j):
        return other * 4 + lax.rem(y + j, 4)

    is_a = f < 2
    is_b = both(f >= 6, f < 8)
    is_c = both(f >= 8, f < 10)
    is_d = f >= 14
    not_b = jnp.logical_or(f < 6, f >= 8)
    not_c = jnp.logical_or(f < 8, f >= 10)
    always = f >= 0
    inner = both(f >= 2, f < 14)
    odd = core == 1
    even = core == 0

    local = []
    for h in range(HEADS_LOCAL):
        cols = pl.ds(h * HEAD_DIM, HEAD_DIM)
        local.append([
            pltpu.make_async_copy(k_hbm.at[:, cols], kv.at[OWN, h, 0], loc.at[3 * h]),
            pltpu.make_async_copy(v_hbm.at[:, cols], kv.at[OWN, h, 1], loc.at[3 * h + 1]),
            pltpu.make_async_copy(q_hbm.at[:, cols], qs.at[h], loc.at[3 * h + 2]),
        ])
    for copies in local:
        for c in copies:
            c.start()
    own_cols = pl.ds(pl.multiple_of(g * ROWS, 128), ROWS)
    w_local = pltpu.make_async_copy(w_hbm.at[:, own_cols], wcol.at[g], loc.at[15])
    hid_local = pltpu.make_async_copy(hid_hbm, hid, loc.at[16])
    mask_local = pltpu.make_async_copy(mask_hbm, mask_s, loc.at[17])
    gate_local = pltpu.make_async_copy(gate_hbm, gate_s, loc.at[18])

    barrier = pltpu.get_barrier_semaphore()
    peers = [
        (always, (sib, g)), (always, (f8, g)),
        (both(f < 14, not_b), (f + 2, g)), (both(f >= 2, not_c), (f - 2, g)),
        (jnp.logical_or(is_a, is_c), (f + 6, g)), (jnp.logical_or(is_b, is_d), (f - 6, g)),
        (always, (f, cross(0))),
    ]
    peers += [(always, (f, same(j))) for j in (1, 2, 3)]
    peers += [(always, (f8, cross(j))) for j in range(4)]
    count = 0
    for cond, dev in peers:
        if cond is always:
            pl.semaphore_signal(barrier, inc=1, device_id=dev, device_id_type=MESH)
            count = count + 1
        else:
            @pl.when(cond)
            def _(dev=dev):
                pl.semaphore_signal(barrier, inc=1, device_id=dev, device_id_type=MESH)
            count = count + jnp.where(cond, 1, 0)
    pl.semaphore_wait(barrier, count)

    edges = [
        (0, always, OWN, SIB, sib),
        (1, both(f < 14, not_b), OWN, LEFT, f + 2),
        (2, both(f >= 2, not_c), OWN, RIGHT, f - 2),
        (3, always, OWN, FAR8, f8),
        (4, jnp.logical_or(both(f >= 2, f < 6), both(f >= 8, f < 12)), LEFT, LEFT2, f + 2),
        (4, is_b, LEFT, RIGHT2, f - 6),
        (5, jnp.logical_or(both(f >= 4, f < 8), both(f >= 10, f < 14)), RIGHT, RIGHT2, f - 2),
        (5, is_c, RIGHT, LEFT2, f + 6),
        (6, both(odd, f >= 2), LEFT, FWD, f - 1),
        (6, both(even, f < 14), RIGHT, FWD, f + 1),
        (7, is_d, FAR8, LEFT, f - 6),
        (7, is_a, FAR8, RIGHT, f + 6),
        (7, both(f >= 12, f < 14), FAR8, RELAY, f + 2),
        (7, both(f >= 2, f < 4), FAR8, RELAY, f - 2),
        (8, is_a, RELAY, RIGHT2, f + 6),
        (8, is_d, RELAY, LEFT2, f - 6),
    ]

    def kv_copy(h, edge):
        kind, _, src, dst, to = edge
        return pltpu.make_async_remote_copy(
            src_ref=kv.at[src, h], dst_ref=kv.at[dst, h],
            send_sem=kv_send.at[kind, h], recv_sem=kv_recv.at[dst, h],
            device_id=(to, g), device_id_type=MESH)

    def kv_start(h, *kinds):
        for edge in edges:
            if edge[0] in kinds:
                if edge[1] is always:
                    kv_copy(h, edge).start()
                else:
                    @pl.when(edge[1])
                    def _(edge=edge):
                        kv_copy(h, edge).start()

    has = {
        SIB: always, FAR8: always, LEFT: f >= 2, RIGHT: f < 14, LEFT2: f >= 4, RIGHT2: f < 12,
        FWD: jnp.logical_or(both(even, f >= 2), both(odd, f < 14)),
        RELAY: jnp.logical_or(is_a, is_d),
    }

    def kv_wait(h, slot):
        def wait():
            pltpu.make_async_remote_copy(
                src_ref=kv.at[slot, h], dst_ref=kv.at[slot, h],
                send_sem=kv_send.at[0, h], recv_sem=kv_recv.at[slot, h],
                device_id=(sib, g), device_id_type=MESH).wait_recv()
        if has[slot] is always:
            wait()
        else:
            pl.when(has[slot])(wait)

    half = pl.ds(pl.multiple_of(core * HALF, 16), HALF)
    w_peers = [(f, same(j)) for j in (1, 2, 3)] + [(f8, cross(j)) for j in range(4)]

    def w_copy(i):
        frame, group = w_peers[i]
        cols = pl.ds(pl.multiple_of(group * ROWS, 128), ROWS)
        return pltpu.make_async_remote_copy(
            src_ref=w_hbm.at[half, cols], dst_ref=wcol.at[g, half],
            send_sem=w_send.at[i], recv_sem=w_recv.at[g],
            device_id=(frame, group), device_id_type=MESH)

    def w_wait(i):
        group = w_peers[i][1]
        pltpu.make_async_remote_copy(
            src_ref=wcol.at[group, half], dst_ref=wcol.at[group, half],
            send_sem=w_send.at[i], recv_sem=w_recv.at[group],
            device_id=(sib, g), device_id_type=MESH).wait_recv()

    def w_forward(i):
        group = w_peers[i][1]
        return pltpu.make_async_remote_copy(
            src_ref=wcol.at[group, half], dst_ref=wcol.at[group, half],
            send_sem=ws_send.at[i], recv_sem=ws_recv.at[group],
            device_id=(sib, g), device_id_type=MESH)

    def ws_wait(i):
        group = w_peers[i][1]
        theirs = pl.ds(pl.multiple_of((1 - core) * HALF, 16), HALF)
        pltpu.make_async_remote_copy(
            src_ref=wcol.at[group, theirs], dst_ref=wcol.at[group, theirs],
            send_sem=ws_send.at[i], recv_sem=ws_recv.at[group],
            device_id=(sib, g), device_id_type=MESH).wait_recv()

    gathers = [
        (0, g, cross(0)), (1, g, same(1)), (2, g, same(3)),
        (3, cross(0), same(1)), (4, cross(0), same(3)),
        (5, same(3), same(1)), (6, cross(1), same(3)),
        (5, g, same(2)), (6, cross(0), same(2)),
    ]
    LAST = HEADS_LOCAL - 1

    def at_copy(h, kind):
        slot, group, to = gathers[kind]
        return pltpu.make_async_remote_copy(
            src_ref=att.at[group, h], dst_ref=att.at[group, h],
            send_sem=at_send.at[slot, h], recv_sem=at_recv.at[group, h],
            device_id=(f, to), device_id_type=MESH)

    def at_wait(h, group):
        pltpu.make_async_remote_copy(
            src_ref=att.at[group, h], dst_ref=att.at[group, h],
            send_sem=at_send.at[0, h], recv_sem=at_recv.at[group, h],
            device_id=(sib, g), device_id_type=MESH).wait_recv()

    def relay_attended(h, last=False):
        h = jnp.int32(h)
        at_wait(h, cross(0))
        at_copy(h, 3).start()
        at_copy(h, 4).start()
        if last:
            at_copy(h, 8).start()
            at_wait(h, same(3))
            at_wait(h, cross(1))
            return
        at_wait(h, same(3))
        at_copy(h, 5).start()
        at_wait(h, cross(1))
        at_copy(h, 6).start()

    def project(h):
        h = jnp.int32(h)
        at_wait(h, same(1))
        at_wait(h, same(2))
        at_wait(h, cross(2))
        at_wait(h, cross(3))
        rows = pl.ds(pl.multiple_of(h * HEAD_DIM, 128), HEAD_DIM)
        lhs = jnp.concatenate([att[i, h] for i in range(GROUPS)], axis=1)
        rhs = jnp.concatenate([wcol[i, rows, :] for i in range(GROUPS)], axis=0)
        proj[...] += jnp.dot(lhs, rhs, preferred_element_type=jnp.float32)

    far_row = {LEFT: 0, RIGHT: 1, FAR8: 2, LEFT2: 3, RIGHT2: 4}

    def attend(h, slot):
        def run():
            s_all = lax.dot_general(
                qs[h], kv[slot, h, 0], (((1,), (1,)), ((), ())),
                preferred_element_type=jnp.float32)
            weights = []
            for b in range(ROWS // BLK):
                rows = slice(b * BLK, (b + 1) * BLK)
                s = s_all[rows]
                if slot in far_row:
                    s = s + bias[far_row[slot], b:b + 1, :]
                top = functools.reduce(
                    jnp.maximum, [s[:, i * 128:(i + 1) * 128] for i in range(5)])
                old = m_s[rows, :]
                new = jnp.maximum(old, jnp.max(top, axis=1, keepdims=True))
                factor = jnp.exp2((old - new) * SCALE2)
                parts = [jnp.exp2((s[:, i * 128:(i + 1) * 128] - new) * SCALE2) for i in range(5)]
                m_s[rows, :] = new
                l_s[rows, :] = l_s[rows, :] * factor + functools.reduce(jnp.add, parts)
                acc[rows, :] = acc[rows, :] * factor
                weights.append(jnp.concatenate([p.astype(jnp.bfloat16) for p in parts], axis=1))
            acc[...] += jnp.dot(
                jnp.concatenate(weights, axis=0), kv[slot, h, 1],
                preferred_element_type=jnp.float32)
        cond = always if slot == OWN else has[slot]
        if cond is always:
            run()
        else:
            pl.when(cond)(run)

    for c in local[0]:
        c.wait()
    kv_start(0, 3)
    kv_start(0, 1, 2, 0)
    for c in local[1]:
        c.wait()
    kv_start(1, 3)
    kv_start(1, 1, 2, 0)
    w_local.start()
    hid_local.start()
    mask_local.start()
    gate_local.start()
    for i in range(7):
        w_copy(i).start()
    for h in range(2, HEADS_LOCAL):
        for c in local[h]:
            c.wait()

    mask_local.wait()
    for a in range(5):
        for b in range(5):
            blocked = (mask_s[a, b].astype(jnp.float32) - 1.0) * (-NEG)
            far8 = jnp.where(f < 8, blocked[:, 5:6], blocked[:, 0:1])
            for slot, column in ((LEFT, blocked[:, 2:3]), (RIGHT, blocked[:, 3:4]), (FAR8, far8),
                                 (LEFT2, blocked[:, 1:2]), (RIGHT2, blocked[:, 4:5])):
                bias[far_row[slot], a:a + 1, b * BLK:(b + 1) * BLK] = jnp.broadcast_to(column, (1, BLK))
    proj[...] = jnp.zeros_like(proj)
    w_local.wait()
    hid_local.wait()
    gate_local.wait()

    def relay_far(h):
        kv_wait(h, FAR8)
        kv_start(h, 7)

    def relay_near(h):
        @pl.when(f < 8)
        def _():
            kv_wait(h, LEFT)
            kv_start(h, 4)
            kv_wait(h, RIGHT)
            kv_start(h, 5, 6)

        @pl.when(f >= 8)
        def _():
            kv_wait(h, RIGHT)
            kv_start(h, 5)
            kv_wait(h, LEFT)
            kv_start(h, 4, 6)

    def step(h, _):
        @pl.when(h < HEADS_LOCAL - 2)
        def _():
            kv_start(h + 2, 1, 2, 0)

        @pl.when(h < HEADS_LOCAL - 3)
        def _():
            relay_far(h + 3)

        m_s[...] = jnp.full_like(m_s, NEG)
        l_s[...] = jnp.zeros_like(l_s)
        acc[...] = jnp.zeros_like(acc)
        attend(h, OWN)
        kv_wait(h, SIB)
        attend(h, SIB)
        attend(h, FAR8)

        @pl.when(h < HEADS_LOCAL - 1)
        def _():
            kv_wait(h + 1, RELAY)
            kv_start(h + 1, 8)
            relay_near(h + 1)

        attend(h, LEFT)
        attend(h, RIGHT)

        kv_wait(h, FWD)
        attend(h, FWD)

        @pl.when(h >= 1)
        def _():
            relay_attended(h - 1)

        @pl.when(h == 2)
        def _():
            for i in range(7):
                w_wait(i)
                w_forward(i).start()

        @pl.when(h == 3)
        def _():
            for i in range(7):
                ws_wait(i)
            project(0)
            project(1)

        @pl.when(h == 4)
        def _():
            project(2)

        kv_wait(h, LEFT2)
        attend(h, LEFT2)
        kv_wait(h, RIGHT2)
        attend(h, RIGHT2)
        total = jnp.sum(l_s[...], axis=1, keepdims=True)
        att[g, h] = (acc[...] / total).astype(jnp.bfloat16)
        at_copy(h, 0).start()
        at_copy(h, 1).start()
        at_copy(h, 2).start()

        @pl.when(h == LAST)
        def _():
            at_copy(h, 7).start()
        return 0

    relay_far(0)
    kv_start(2, 3)
    relay_far(1)
    kv_start(3, 3)
    relay_near(0)
    kv_wait(0, RELAY)
    kv_start(0, 8)
    relay_far(2)
    kv_start(4, 3)
    lax.fori_loop(0, HEADS_LOCAL, step, 0)
    project(3)
    relay_attended(LAST, last=True)
    project(4)
    gate = gate_s[pl.ds(ts_ref[0], 1), :]
    out_ref[...] = (hid[...].astype(jnp.float32) + gate * proj[...]).astype(out_ref.dtype)

    def drain(h, _):
        for edge in edges:
            if edge[1] is always:
                kv_copy(h, edge).wait_send()
            else:
                @pl.when(edge[1])
                def _(edge=edge):
                    kv_copy(h, edge).wait_send()
        for kind in range(7):
            at_copy(h, kind).wait_send()
        return 0

    lax.fori_loop(0, HEADS_LOCAL, drain, 0)
    for i in range(7):
        w_copy(i).wait_send()
        w_forward(i).wait_send()


def body(hidden_in, queries, keys, values, radial_mask, out_weight, gate_table, timestep):
    any_spec = pl.BlockSpec(memory_space=pl.ANY)
    dma = pltpu.SemaphoreType.DMA
    return pl.pallas_call(
        kernel,
        out_shape=jax.ShapeDtypeStruct((ROWS, ROWS), jnp.bfloat16),
        in_specs=[
            pl.BlockSpec(memory_space=pltpu.SMEM),
            any_spec, any_spec, any_spec, any_spec, any_spec, any_spec, any_spec,
        ],
        out_specs=pl.BlockSpec(memory_space=pltpu.VMEM),
        scratch_shapes=[
            pltpu.VMEM((SLOTS, HEADS_LOCAL, 2, ROWS, HEAD_DIM), jnp.bfloat16),
            pltpu.VMEM((HEADS_LOCAL, ROWS, HEAD_DIM), jnp.bfloat16),
            pltpu.VMEM((GROUPS, HEADS_LOCAL, ROWS, HEAD_DIM), jnp.bfloat16),
            pltpu.VMEM((GROUPS, ROWS, ROWS), jnp.bfloat16),
            pltpu.VMEM((ROWS, ROWS), jnp.bfloat16),
            pltpu.VMEM((5, 5, 1, 6), jnp.int32),
            pltpu.VMEM((50, ROWS), jnp.float32),
            pltpu.VMEM((5, 5, ROWS), jnp.float32),
            pltpu.VMEM((ROWS, HEAD_DIM), jnp.float32),
            pltpu.VMEM((ROWS, HEAD_DIM), jnp.float32),
            pltpu.VMEM((ROWS, HEAD_DIM), jnp.float32),
            pltpu.VMEM((ROWS, ROWS), jnp.float32),
            dma((19,)),
            dma((9, HEADS_LOCAL)), dma((SLOTS, HEADS_LOCAL)),
            dma((7, HEADS_LOCAL)), dma((GROUPS, HEADS_LOCAL)),
            dma((7,)), dma((GROUPS,)), dma((7,)), dma((GROUPS,)),
        ],
        compiler_params=pltpu.CompilerParams(
            collective_id=0, has_side_effects=True, vmem_limit_bytes=60 * 1024 * 1024),
        cost_estimate=pl.CostEstimate(
            flops=14_000_000_000, bytes_accessed=12_000_000, transcendentals=16_000_000),
    )(timestep, radial_mask.transpose(2, 3, 0, 1), gate_table, hidden_in, queries, keys, values, out_weight)


def solution(mesh):
    in_specs = (
        P("frame", "head"), P("frame", "head"), P("frame", "head"), P("frame", "head"),
        P("frame", None, None, None), P("head", None), P(None, "head"), P(),
    )
    return jax.shard_map(
        body, mesh=mesh, in_specs=in_specs, out_specs=P("frame", "head"), check_vma=False)
```

```python
import functools

import jax
import jax.numpy as jnp
from jax import lax
from jax.experimental import pallas as pl
from jax.experimental.pallas import tpu as pltpu
from jax.sharding import PartitionSpec as P

MESH = pl.DeviceIdType.MESH
HEAD_DIM = 128
BLK = 128
ROWS = 640
HEADS_LOCAL = 5
GROUPS = 8
SLOTS = 9
OWN, SIB, LEFT, RIGHT, FAR8, FWD, LEFT2, RIGHT2, RELAY = range(9)
SCALE2 = 1.4426950408889634 * HEAD_DIM ** -0.5
NEG = -1e30
QUARTER = ROWS // 4
PASSED = ((0, 2), (1, 3), (4, 6), (5,))


def both(*conds):
    out = conds[0]
    for c in conds[1:]:
        out = jnp.logical_and(out, c)
    return out


def kernel(ts_ref, mask_hbm, gate_hbm, hid_hbm, q_hbm, k_hbm, v_hbm, w_hbm, out_ref,
           kv, qs, att, wcol, hid, mask_s, gate_s, bias, m_s, l_s, acc, proj,
           loc, kv_send, kv_recv, at_send, at_recv, w_send, w_recv, ws_send, ws_recv):
    f = lax.axis_index("frame")
    g = lax.axis_index("head")
    core = lax.rem(f, 2)
    sib = f + 1 - 2 * core
    f8 = lax.rem(f + 8, 16)
    zh = g // 4
    zl = f // 8
    y = lax.rem(g, 4)
    other = 1 - zh

    def same(j):
        return zh * 4 + lax.rem(y + j, 4)

    def cross(j):
        return other * 4 + lax.rem(y + j, 4)

    is_a = f < 2
    is_b = both(f >= 6, f < 8)
    is_c = both(f >= 8, f < 10)
    is_d = f >= 14
    not_b = jnp.logical_or(f < 6, f >= 8)
    not_c = jnp.logical_or(f < 8, f >= 10)
    always = f >= 0
    middle = both(f >= 6, f < 10)
    inner = both(f >= 2, f < 14)
    odd = core == 1
    even = core == 0

    local = []
    for h in range(HEADS_LOCAL):
        cols = pl.ds(h * HEAD_DIM, HEAD_DIM)
        local.append([
            pltpu.make_async_copy(k_hbm.at[:, cols], kv.at[OWN, h, 0], loc.at[3 * h]),
            pltpu.make_async_copy(v_hbm.at[:, cols], kv.at[OWN, h, 1], loc.at[3 * h + 1]),
            pltpu.make_async_copy(q_hbm.at[:, cols], qs.at[h], loc.at[3 * h + 2]),
        ])
    for copies in local:
        for c in copies:
            c.start()
    own_cols = pl.ds(pl.multiple_of(g * ROWS, 128), ROWS)
    w_local = pltpu.make_async_copy(w_hbm.at[:, own_cols], wcol.at[g], loc.at[15])
    hid_local = pltpu.make_async_copy(hid_hbm, hid, loc.at[16])
    mask_local = pltpu.make_async_copy(mask_hbm, mask_s, loc.at[17])
    gate_local = pltpu.make_async_copy(gate_hbm, gate_s, loc.at[18])

    barrier = pltpu.get_barrier_semaphore()
    peers = [
        (always, (sib, g)), (always, (f8, g)),
        (both(f < 14, not_b), (f + 2, g)), (both(f >= 2, not_c), (f - 2, g)),
        (jnp.logical_or(is_a, is_c), (f + 6, g)), (jnp.logical_or(is_b, is_d), (f - 6, g)),
        (always, (f, cross(0))),
    ]
    peers += [(always, (f, same(j))) for j in (1, 2, 3)]
    peers += [(always, (f8, cross(j))) for j in range(4)]
    count = 0
    for cond, dev in peers:
        if cond is always:
            pl.semaphore_signal(barrier, inc=1, device_id=dev, device_id_type=MESH)
            count = count + 1
        else:
            @pl.when(cond)
            def _(dev=dev):
                pl.semaphore_signal(barrier, inc=1, device_id=dev, device_id_type=MESH)
            count = count + jnp.where(cond, 1, 0)
    pl.semaphore_wait(barrier, count)

    edges = [
        (0, always, OWN, SIB, sib),
        (1, both(f < 14, not_b), OWN, LEFT, f + 2),
        (2, both(f >= 2, not_c), OWN, RIGHT, f - 2),
        (3, always, OWN, FAR8, f8),
        (4, jnp.logical_or(both(f >= 2, f < 6), both(f >= 8, f < 12)), LEFT, LEFT2, f + 2),
        (4, is_b, LEFT, RIGHT2, f - 6),
        (5, jnp.logical_or(both(f >= 4, f < 8), both(f >= 10, f < 14)), RIGHT, RIGHT2, f - 2),
        (5, is_c, RIGHT, LEFT2, f + 6),
        (6, both(odd, f >= 2), LEFT, FWD, f - 1),
        (6, both(even, f < 14), RIGHT, FWD, f + 1),
        (7, is_d, FAR8, LEFT, f - 6),
        (7, is_a, FAR8, RIGHT, f + 6),
        (7, both(f >= 12, f < 14), FAR8, RELAY, f + 2),
        (7, both(f >= 2, f < 4), FAR8, RELAY, f - 2),
        (8, is_a, RELAY, RIGHT2, f + 6),
        (8, is_d, RELAY, LEFT2, f - 6),
    ]

    def kv_copy(h, edge):
        kind, _, src, dst, to = edge
        return pltpu.make_async_remote_copy(
            src_ref=kv.at[src, h], dst_ref=kv.at[dst, h],
            send_sem=kv_send.at[kind, h], recv_sem=kv_recv.at[dst, h],
            device_id=(to, g), device_id_type=MESH)

    def kv_start(h, *kinds):
        for edge in edges:
            if edge[0] in kinds:
                if edge[1] is always:
                    kv_copy(h, edge).start()
                else:
                    @pl.when(edge[1])
                    def _(edge=edge):
                        kv_copy(h, edge).start()

    has = {
        SIB: always, FAR8: always, LEFT: f >= 2, RIGHT: f < 14, LEFT2: f >= 4, RIGHT2: f < 12,
        FWD: jnp.logical_or(both(even, f >= 2), both(odd, f < 14)),
        RELAY: jnp.logical_or(is_a, is_d),
    }

    def kv_wait(h, slot):
        def wait():
            pltpu.make_async_remote_copy(
                src_ref=kv.at[slot, h], dst_ref=kv.at[slot, h],
                send_sem=kv_send.at[0, h], recv_sem=kv_recv.at[slot, h],
                device_id=(sib, g), device_id_type=MESH).wait_recv()
        if has[slot] is always:
            wait()
        else:
            pl.when(has[slot])(wait)

    def quarter(on_core, on_zl):
        return pl.ds(pl.multiple_of((on_core * 2 + on_zl) * QUARTER, 16), QUARTER)

    w_peers = [(f, same(j), zl) for j in (1, 2, 3)] + [(f8, cross(j), 1 - zl) for j in range(4)]

    def w_copy(i):
        frame, group, their_zl = w_peers[i]
        cols = pl.ds(pl.multiple_of(group * ROWS, 128), ROWS)
        rows = quarter(core, their_zl)
        return pltpu.make_async_remote_copy(
            src_ref=w_hbm.at[rows, cols], dst_ref=wcol.at[g, rows],
            send_sem=w_send.at[i], recv_sem=w_recv.at[g],
            device_id=(frame, group), device_id_type=MESH)

    def w_pass(i, kind):
        group = w_peers[i][1]
        rows = quarter(core, zl if kind < 2 else 1 - zl)
        return pltpu.make_async_remote_copy(
            src_ref=wcol.at[group, rows], dst_ref=wcol.at[group, rows],
            send_sem=ws_send.at[kind, i], recv_sem=ws_recv.at[kind, group],
            device_id=(f8 if kind == 1 else sib, g), device_id_type=MESH)

    def w_wait(i):
        group = w_peers[i][1]
        ref = wcol.at[group, quarter(core, zl)]
        pltpu.make_async_remote_copy(
            src_ref=ref, dst_ref=ref, send_sem=w_send.at[i], recv_sem=w_recv.at[group],
            device_id=(sib, g), device_id_type=MESH).wait_recv()

    def ws_wait(i, kind):
        group = w_peers[i][1]
        ref = wcol.at[group, quarter(core if kind == 1 else 1 - core, zl if kind == 0 else 1 - zl)]
        pltpu.make_async_remote_copy(
            src_ref=ref, dst_ref=ref, send_sem=ws_send.at[kind, i], recv_sem=ws_recv.at[kind, group],
            device_id=(sib, g), device_id_type=MESH).wait_recv()

    gathers = [
        (0, g, cross(0)), (1, g, same(1)), (2, g, same(3)),
        (3, cross(0), same(1)), (4, cross(0), same(3)),
        (5, same(3), same(1)), (6, cross(1), same(3)),
        (5, g, same(2)), (6, cross(0), same(2)),
    ]
    LAST = HEADS_LOCAL - 1
    DIRECT = HEADS_LOCAL - 1

    def at_copy(h, kind):
        slot, group, to = gathers[kind]
        return pltpu.make_async_remote_copy(
            src_ref=att.at[group, h], dst_ref=att.at[group, h],
            send_sem=at_send.at[slot, h], recv_sem=at_recv.at[group, h],
            device_id=(f, to), device_id_type=MESH)

    def at_wait(h, group):
        pltpu.make_async_remote_copy(
            src_ref=att.at[group, h], dst_ref=att.at[group, h],
            send_sem=at_send.at[0, h], recv_sem=at_recv.at[group, h],
            device_id=(sib, g), device_id_type=MESH).wait_recv()

    def relay_partner(h):
        h = jnp.int32(h)
        at_wait(h, cross(0))
        at_copy(h, 3).start()
        at_copy(h, 4).start()

        @pl.when(h >= DIRECT)
        def _():
            at_copy(h, 8).start()

    def relay_same(h):
        h = jnp.int32(h)
        at_wait(h, same(3))
        at_copy(h, 5).start()

    def relay_cross(h):
        h = jnp.int32(h)
        at_wait(h, cross(1))
        at_copy(h, 6).start()

    def add_projected(h, groups):
        rows = pl.ds(pl.multiple_of(h * HEAD_DIM, 128), HEAD_DIM)
        lhs = jnp.concatenate([att[i, h] for i in groups], axis=1)
        rhs = jnp.concatenate([wcol[i, rows, :] for i in groups], axis=0)
        proj[...] += jnp.dot(lhs, rhs, preferred_element_type=jnp.float32)

    def project(h):
        if h >= DIRECT:
            at_wait(jnp.int32(h), same(3))
            at_wait(jnp.int32(h), cross(1))
        h = jnp.int32(h)
        at_wait(h, same(1))
        at_wait(h, same(2))
        at_wait(h, cross(2))
        at_wait(h, cross(3))
        add_projected(h, range(GROUPS))

    def project_last():
        h = jnp.int32(LAST)
        for j in (1, 3, 2):
            at_wait(h, same(j))
        add_projected(h, [g, same(1), same(2), same(3)])
        for j in (1, 3, 2):
            at_wait(h, cross(j))
        add_projected(h, [cross(j) for j in range(4)])

    far_row = {LEFT: 0, RIGHT: 1, FAR8: 2, LEFT2: 3, RIGHT2: 4}

    def attend(h, slot):
        def run():
            s_all = lax.dot_general(
                qs[h], kv[slot, h, 0], (((1,), (1,)), ((), ())),
                preferred_element_type=jnp.float32)
            weights = []
            for b in range(ROWS // BLK):
                rows = slice(b * BLK, (b + 1) * BLK)
                s = s_all[rows]
                if slot in far_row:
                    s = s + bias[far_row[slot], b:b + 1, :]
                top = functools.reduce(
                    jnp.maximum, [s[:, i * 128:(i + 1) * 128] for i in range(5)])
                old = m_s[rows, :]
                new = jnp.maximum(old, jnp.max(top, axis=1, keepdims=True))
                factor = jnp.exp2((old - new) * SCALE2)
                parts = [jnp.exp2((s[:, i * 128:(i + 1) * 128] - new) * SCALE2) for i in range(5)]
                m_s[rows, :] = new
                l_s[rows, :] = l_s[rows, :] * factor + functools.reduce(jnp.add, parts)
                acc[rows, :] = acc[rows, :] * factor
                weights.append(jnp.concatenate([p.astype(jnp.bfloat16) for p in parts], axis=1))
            acc[...] += jnp.dot(
                jnp.concatenate(weights, axis=0), kv[slot, h, 1],
                preferred_element_type=jnp.float32)
        cond = always if slot == OWN else has[slot]
        if cond is always:
            run()
        else:
            pl.when(cond)(run)

    for c in local[0]:
        c.wait()
    kv_start(0, 3)
    kv_start(0, 1, 2, 0)
    for c in local[1]:
        c.wait()
    kv_start(1, 3)
    kv_start(1, 1, 2, 0)
    w_local.start()
    hid_local.start()
    mask_local.start()
    gate_local.start()
    for i in range(7):
        w_copy(i).start()
    for h in range(2, HEADS_LOCAL):
        for c in local[h]:
            c.wait()

    mask_local.wait()
    for a in range(5):
        for b in range(5):
            blocked = (mask_s[a, b].astype(jnp.float32) - 1.0) * (-NEG)
            far8 = jnp.where(f < 8, blocked[:, 5:6], blocked[:, 0:1])
            for slot, column in ((LEFT, blocked[:, 2:3]), (RIGHT, blocked[:, 3:4]), (FAR8, far8),
                                 (LEFT2, blocked[:, 1:2]), (RIGHT2, blocked[:, 4:5])):
                bias[far_row[slot], a:a + 1, b * BLK:(b + 1) * BLK] = jnp.broadcast_to(column, (1, BLK))
    proj[...] = jnp.zeros_like(proj)
    w_local.wait()
    hid_local.wait()
    gate_local.wait()

    def relay_far(h):
        kv_wait(h, FAR8)
        kv_start(h, 7)

    def relay_near(h):
        @pl.when(f < 8)
        def _():
            kv_wait(h, LEFT)
            kv_start(h, 4)
            kv_wait(h, RIGHT)
            kv_start(h, 5, 6)

        @pl.when(f >= 8)
        def _():
            kv_wait(h, RIGHT)
            kv_start(h, 5)
            kv_wait(h, LEFT)
            kv_start(h, 4, 6)

    def step(h, _):
        @pl.when(both(h < HEADS_LOCAL - 2, jnp.logical_or(h > 0, jnp.logical_not(middle))))
        def _():
            kv_start(h + 2, 1, 2, 0)

        @pl.when(h < HEADS_LOCAL - 3)
        def _():
            relay_far(h + 3)

        m_s[...] = jnp.full_like(m_s, NEG)
        l_s[...] = jnp.zeros_like(l_s)
        acc[...] = jnp.zeros_like(acc)
        attend(h, OWN)
        kv_wait(h, SIB)
        attend(h, SIB)
        attend(h, FAR8)

        @pl.when(h < HEADS_LOCAL - 1)
        def _():
            kv_wait(h + 1, RELAY)
            kv_start(h + 1, 8)
            relay_near(h + 1)

        @pl.when(both(h >= 2, h < DIRECT + 2))
        def _():
            relay_cross(h - 2)

        attend(h, LEFT)
        attend(h, RIGHT)
        kv_wait(h, FWD)
        attend(h, FWD)

        @pl.when(h >= 1)
        def _():
            relay_partner(h - 1)

        @pl.when(both(h >= 1, h < DIRECT + 1))
        def _():
            relay_same(h - 1)

        @pl.when(h == LAST)
        def _():
            for i in range(7):
                ws_wait(i, 1)
                w_pass(i, 2).start()

        kv_wait(h, LEFT2)
        attend(h, LEFT2)
        kv_wait(h, RIGHT2)
        attend(h, RIGHT2)
        total = jnp.sum(l_s[...], axis=1, keepdims=True)
        att[g, h] = (acc[...] / total).astype(jnp.bfloat16)
        at_copy(h, 0).start()
        at_copy(h, 1).start()
        at_copy(h, 2).start()

        @pl.when(h >= DIRECT)
        def _():
            at_copy(h, 7).start()

        for after, blocks in enumerate(PASSED):
            @pl.when(h == after)
            def _(blocks=blocks):
                for i in blocks:
                    w_wait(i)
                    w_pass(i, 0).start()
                    w_pass(i, 1).start()

        return 0

    relay_far(0)
    kv_start(2, 3)
    relay_far(1)
    kv_start(3, 3)

    @pl.when(middle)
    def _():
        kv_start(2, 1, 2, 0)

    relay_near(0)
    kv_wait(0, RELAY)
    kv_start(0, 8)
    relay_far(2)
    kv_start(4, 3)
    lax.fori_loop(0, HEADS_LOCAL, step, 0)
    relay_partner(LAST)
    for i in range(7):
        ws_wait(i, 0)
        ws_wait(i, 2)
    relay_cross(3)
    for h in range(LAST):
        project(h)
    project_last()
    gate = gate_s[pl.ds(ts_ref[0], 1), :]
    out_ref[...] = (hid[...].astype(jnp.float32) + gate * proj[...]).astype(out_ref.dtype)

    def drain(h, _):
        for edge in edges:
            if edge[1] is always:
                kv_copy(h, edge).wait_send()
            else:
                @pl.when(edge[1])
                def _(edge=edge):
                    kv_copy(h, edge).wait_send()
        for kind in range(7):
            at_copy(h, kind).wait_send()
        return 0

    lax.fori_loop(0, HEADS_LOCAL, drain, 0)
    for i in range(7):
        w_copy(i).wait_send()
        for kind in range(3):
            w_pass(i, kind).wait_send()


def body(hidden_in, queries, keys, values, radial_mask, out_weight, gate_table, timestep):
    any_spec = pl.BlockSpec(memory_space=pl.ANY)
    dma = pltpu.SemaphoreType.DMA
    return pl.pallas_call(
        kernel,
        out_shape=jax.ShapeDtypeStruct((ROWS, ROWS), jnp.bfloat16),
        in_specs=[
            pl.BlockSpec(memory_space=pltpu.SMEM),
            any_spec, any_spec, any_spec, any_spec, any_spec, any_spec, any_spec,
        ],
        out_specs=pl.BlockSpec(memory_space=pltpu.VMEM),
        scratch_shapes=[
            pltpu.VMEM((SLOTS, HEADS_LOCAL, 2, ROWS, HEAD_DIM), jnp.bfloat16),
            pltpu.VMEM((HEADS_LOCAL, ROWS, HEAD_DIM), jnp.bfloat16),
            pltpu.VMEM((GROUPS, HEADS_LOCAL, ROWS, HEAD_DIM), jnp.bfloat16),
            pltpu.VMEM((GROUPS, ROWS, ROWS), jnp.bfloat16),
            pltpu.VMEM((ROWS, ROWS), jnp.bfloat16),
            pltpu.VMEM((5, 5, 1, 6), jnp.int32),
            pltpu.VMEM((50, ROWS), jnp.float32),
            pltpu.VMEM((5, 5, ROWS), jnp.float32),
            pltpu.VMEM((ROWS, HEAD_DIM), jnp.float32),
            pltpu.VMEM((ROWS, HEAD_DIM), jnp.float32),
            pltpu.VMEM((ROWS, HEAD_DIM), jnp.float32),
            pltpu.VMEM((ROWS, ROWS), jnp.float32),
            dma((19,)),
            dma((9, HEADS_LOCAL)), dma((SLOTS, HEADS_LOCAL)),
            dma((7, HEADS_LOCAL)), dma((GROUPS, HEADS_LOCAL)),
            dma((7,)), dma((GROUPS,)), dma((3, 7)), dma((3, GROUPS)),
        ],
        compiler_params=pltpu.CompilerParams(
            collective_id=0, has_side_effects=True, vmem_limit_bytes=60 * 1024 * 1024),
        cost_estimate=pl.CostEstimate(
            flops=14_000_000_000, bytes_accessed=12_000_000, transcendentals=16_000_000),
    )(timestep, radial_mask.transpose(2, 3, 0, 1), gate_table, hidden_in, queries, keys, values, out_weight)


def solution(mesh):
    in_specs = (
        P("frame", "head"), P("frame", "head"), P("frame", "head"), P("frame", "head"),
        P("frame", None, None, None), P("head", None), P(None, "head"), P(),
    )
    return jax.shard_map(
        body, mesh=mesh, in_specs=in_specs, out_specs=P("frame", "head"), check_vma=False)
```

```python
import functools

import jax
import jax.numpy as jnp
from jax import lax
from jax.experimental import pallas as pl
from jax.experimental.pallas import tpu as pltpu
from jax.sharding import PartitionSpec as P

MESH = pl.DeviceIdType.MESH
HEAD_DIM = 128
BLK = 128
ROWS = 640
HEADS_LOCAL = 5
GROUPS = 8
SLOTS = 9
OWN, SIB, LEFT, RIGHT, FAR8, FWD, LEFT2, RIGHT2, RELAY = range(9)
SCALE2 = 1.4426950408889634 * HEAD_DIM ** -0.5
NEG = -1e30
HALF = ROWS // 2
QUARTER = ROWS // 4
SHARED = (1, 5)
PASSED = ((), (1, 5), (0, 2, 3), (4, 6))


def both(*conds):
    out = conds[0]
    for c in conds[1:]:
        out = jnp.logical_and(out, c)
    return out


def kernel(ts_ref, mask_hbm, gate_hbm, hid_hbm, q_hbm, k_hbm, v_hbm, w_hbm, out_ref,
           kv, qs, att, wcol, hid, mask_s, gate_s, bias, m_s, l_s, acc, proj,
           loc, kv_send, kv_recv, at_send, at_recv, w_send, w_recv, ws_send, ws_recv):
    f = lax.axis_index("frame")
    g = lax.axis_index("head")
    core = lax.rem(f, 2)
    sib = f + 1 - 2 * core
    f8 = lax.rem(f + 8, 16)
    zh = g // 4
    zl = f // 8
    y = lax.rem(g, 4)
    other = 1 - zh

    def same(j):
        return zh * 4 + lax.rem(y + j, 4)

    def cross(j):
        return other * 4 + lax.rem(y + j, 4)

    is_a = f < 2
    is_b = both(f >= 6, f < 8)
    is_c = both(f >= 8, f < 10)
    is_d = f >= 14
    not_b = jnp.logical_or(f < 6, f >= 8)
    not_c = jnp.logical_or(f < 8, f >= 10)
    always = f >= 0
    middle = both(f >= 6, f < 10)
    inner = both(f >= 2, f < 14)
    odd = core == 1
    even = core == 0

    local = []
    for h in range(HEADS_LOCAL):
        cols = pl.ds(h * HEAD_DIM, HEAD_DIM)
        local.append([
            pltpu.make_async_copy(k_hbm.at[:, cols], kv.at[OWN, h, 0], loc.at[3 * h]),
            pltpu.make_async_copy(v_hbm.at[:, cols], kv.at[OWN, h, 1], loc.at[3 * h + 1]),
            pltpu.make_async_copy(q_hbm.at[:, cols], qs.at[h], loc.at[3 * h + 2]),
        ])
    for copies in local:
        for c in copies:
            c.start()
    own_cols = pl.ds(pl.multiple_of(g * ROWS, 128), ROWS)
    w_local = pltpu.make_async_copy(w_hbm.at[:, own_cols], wcol.at[g], loc.at[15])
    hid_local = pltpu.make_async_copy(hid_hbm, hid, loc.at[16])
    mask_local = pltpu.make_async_copy(mask_hbm, mask_s, loc.at[17])
    gate_local = pltpu.make_async_copy(gate_hbm, gate_s, loc.at[18])

    barrier = pltpu.get_barrier_semaphore()
    peers = [
        (always, (sib, g)), (always, (f8, g)),
        (both(f < 14, not_b), (f + 2, g)), (both(f >= 2, not_c), (f - 2, g)),
        (jnp.logical_or(is_a, is_c), (f + 6, g)), (jnp.logical_or(is_b, is_d), (f - 6, g)),
        (always, (f, cross(0))),
    ]
    peers += [(always, (f, same(j))) for j in (1, 2, 3)]
    peers += [(always, (f8, cross(j))) for j in range(4)]
    count = 0
    for cond, dev in peers:
        if cond is always:
            pl.semaphore_signal(barrier, inc=1, device_id=dev, device_id_type=MESH)
            count = count + 1
        else:
            @pl.when(cond)
            def _(dev=dev):
                pl.semaphore_signal(barrier, inc=1, device_id=dev, device_id_type=MESH)
            count = count + jnp.where(cond, 1, 0)
    pl.semaphore_wait(barrier, count)

    edges = [
        (0, always, OWN, SIB, sib),
        (1, both(f < 14, not_b), OWN, LEFT, f + 2),
        (2, both(f >= 2, not_c), OWN, RIGHT, f - 2),
        (3, always, OWN, FAR8, f8),
        (4, jnp.logical_or(both(f >= 2, f < 6), both(f >= 8, f < 12)), LEFT, LEFT2, f + 2),
        (4, is_b, LEFT, RIGHT2, f - 6),
        (5, jnp.logical_or(both(f >= 4, f < 8), both(f >= 10, f < 14)), RIGHT, RIGHT2, f - 2),
        (5, is_c, RIGHT, LEFT2, f + 6),
        (6, both(odd, f >= 2), LEFT, FWD, f - 1),
        (6, both(even, f < 14), RIGHT, FWD, f + 1),
        (7, is_d, FAR8, LEFT, f - 6),
        (7, is_a, FAR8, RIGHT, f + 6),
        (7, both(f >= 12, f < 14), FAR8, RELAY, f + 2),
        (7, both(f >= 2, f < 4), FAR8, RELAY, f - 2),
        (8, is_a, RELAY, RIGHT2, f + 6),
        (8, is_d, RELAY, LEFT2, f - 6),
    ]

    def kv_copy(h, edge):
        kind, _, src, dst, to = edge
        return pltpu.make_async_remote_copy(
            src_ref=kv.at[src, h], dst_ref=kv.at[dst, h],
            send_sem=kv_send.at[kind, h], recv_sem=kv_recv.at[dst, h],
            device_id=(to, g), device_id_type=MESH)

    def kv_start(h, *kinds):
        for edge in edges:
            if edge[0] in kinds:
                if edge[1] is always:
                    kv_copy(h, edge).start()
                else:
                    @pl.when(edge[1])
                    def _(edge=edge):
                        kv_copy(h, edge).start()

    has = {
        SIB: always, FAR8: always, LEFT: f >= 2, RIGHT: f < 14, LEFT2: f >= 4, RIGHT2: f < 12,
        FWD: jnp.logical_or(both(even, f >= 2), both(odd, f < 14)),
        RELAY: jnp.logical_or(is_a, is_d),
    }

    def kv_wait_any(h, slot):
        pltpu.make_async_remote_copy(
            src_ref=kv.at[slot, h], dst_ref=kv.at[slot, h],
            send_sem=kv_send.at[0, h], recv_sem=kv_recv.at[slot, h],
            device_id=(sib, g), device_id_type=MESH).wait_recv()

    def kv_wait(h, slot):
        def wait():
            kv_wait_any(h, slot)
        if has[slot] is always:
            wait()
        else:
            pl.when(has[slot])(wait)

    def portion(i, on_core, on_zl):
        if i in SHARED:
            return pl.ds(pl.multiple_of((on_core * 2 + on_zl) * QUARTER, 16), QUARTER)
        return pl.ds(pl.multiple_of(on_core * HALF, 16), HALF)

    w_peers = [(f, same(j), zl) for j in (1, 2, 3)] + [(f8, cross(j), 1 - zl) for j in range(4)]

    def w_copy(i):
        frame, group, their_zl = w_peers[i]
        cols = pl.ds(pl.multiple_of(group * ROWS, 128), ROWS)
        rows = portion(i, core, their_zl)
        return pltpu.make_async_remote_copy(
            src_ref=w_hbm.at[rows, cols], dst_ref=wcol.at[g, rows],
            send_sem=w_send.at[i], recv_sem=w_recv.at[g],
            device_id=(frame, group), device_id_type=MESH)

    def w_pass(i, kind):
        group = w_peers[i][1]
        rows = portion(i, core, zl if kind < 2 else 1 - zl)
        return pltpu.make_async_remote_copy(
            src_ref=wcol.at[group, rows], dst_ref=wcol.at[group, rows],
            send_sem=ws_send.at[kind, i], recv_sem=ws_recv.at[kind, group],
            device_id=(f8 if kind == 1 else sib, g), device_id_type=MESH)

    def w_wait(i):
        group = w_peers[i][1]
        ref = wcol.at[group, portion(i, core, zl)]
        pltpu.make_async_remote_copy(
            src_ref=ref, dst_ref=ref, send_sem=w_send.at[i], recv_sem=w_recv.at[group],
            device_id=(sib, g), device_id_type=MESH).wait_recv()

    def ws_wait(i, kind):
        group = w_peers[i][1]
        ref = wcol.at[group, portion(i, core if kind == 1 else 1 - core, zl if kind == 0 else 1 - zl)]
        pltpu.make_async_remote_copy(
            src_ref=ref, dst_ref=ref, send_sem=ws_send.at[kind, i], recv_sem=ws_recv.at[kind, group],
            device_id=(sib, g), device_id_type=MESH).wait_recv()

    gathers = [
        (0, g, cross(0)), (1, g, same(1)), (2, g, same(3)),
        (3, cross(0), same(1)), (4, cross(0), same(3)),
        (5, same(3), same(1)), (6, cross(1), same(3)),
        (5, g, same(2)), (6, cross(0), same(2)),
    ]
    LAST = HEADS_LOCAL - 1
    DIRECT = HEADS_LOCAL - 1

    def at_copy(h, kind):
        slot, group, to = gathers[kind]
        return pltpu.make_async_remote_copy(
            src_ref=att.at[group, h], dst_ref=att.at[group, h],
            send_sem=at_send.at[slot, h], recv_sem=at_recv.at[group, h],
            device_id=(f, to), device_id_type=MESH)

    def at_wait(h, group):
        pltpu.make_async_remote_copy(
            src_ref=att.at[group, h], dst_ref=att.at[group, h],
            send_sem=at_send.at[0, h], recv_sem=at_recv.at[group, h],
            device_id=(sib, g), device_id_type=MESH).wait_recv()

    def relay_partner(h):
        h = jnp.int32(h)
        at_wait(h, cross(0))
        at_copy(h, 3).start()
        at_copy(h, 4).start()

        @pl.when(h >= DIRECT)
        def _():
            at_copy(h, 8).start()

    def relay_same(h):
        h = jnp.int32(h)
        at_wait(h, same(3))
        at_copy(h, 5).start()

    def relay_cross(h):
        h = jnp.int32(h)
        at_wait(h, cross(1))
        at_copy(h, 6).start()

    def add_projected(h, groups):
        rows = pl.ds(pl.multiple_of(h * HEAD_DIM, 128), HEAD_DIM)
        lhs = jnp.concatenate([att[i, h] for i in groups], axis=1)
        rhs = jnp.concatenate([wcol[i, rows, :] for i in groups], axis=0)
        proj[...] += jnp.dot(lhs, rhs, preferred_element_type=jnp.float32)

    def project(h):
        if h >= DIRECT:
            at_wait(jnp.int32(h), same(3))
            at_wait(jnp.int32(h), cross(1))
        h = jnp.int32(h)
        at_wait(h, same(1))
        at_wait(h, same(2))
        at_wait(h, cross(2))
        at_wait(h, cross(3))
        add_projected(h, range(GROUPS))

    def project_last():
        h = jnp.int32(LAST)
        for j in (1, 3, 2):
            at_wait(h, same(j))
        add_projected(h, [g, same(1), same(2), same(3)])
        for j in (1, 3, 2):
            at_wait(h, cross(j))
        add_projected(h, [cross(j) for j in range(4)])

    far_row = {LEFT: 0, RIGHT: 1, FAR8: 2, LEFT2: 3, RIGHT2: 4}

    def attend(h, slot, row=None, cond=None):
        if cond is None:
            row = far_row.get(slot)
            cond = always if slot == OWN else has[slot]

        def run():
            s_all = lax.dot_general(
                qs[h], kv[slot, h, 0], (((1,), (1,)), ((), ())),
                preferred_element_type=jnp.float32)
            weights = []
            for b in range(ROWS // BLK):
                rows = slice(b * BLK, (b + 1) * BLK)
                s = s_all[rows]
                if row is not None:
                    s = s + bias[row, b:b + 1, :]
                top = functools.reduce(
                    jnp.maximum, [s[:, i * 128:(i + 1) * 128] for i in range(5)])
                old = m_s[rows, :]
                new = jnp.maximum(old, jnp.max(top, axis=1, keepdims=True))
                factor = jnp.exp2((old - new) * SCALE2)
                parts = [jnp.exp2((s[:, i * 128:(i + 1) * 128] - new) * SCALE2) for i in range(5)]
                m_s[rows, :] = new
                l_s[rows, :] = l_s[rows, :] * factor + functools.reduce(jnp.add, parts)
                acc[rows, :] = acc[rows, :] * factor
                weights.append(jnp.concatenate([p.astype(jnp.bfloat16) for p in parts], axis=1))
            acc[...] += jnp.dot(
                jnp.concatenate(weights, axis=0), kv[slot, h, 1],
                preferred_element_type=jnp.float32)
        if cond is always:
            run()
        else:
            pl.when(cond)(run)

    for c in local[0]:
        c.wait()
    kv_start(0, 3)
    kv_start(0, 1, 2, 0)
    for c in local[1]:
        c.wait()
    kv_start(1, 3)
    kv_start(1, 1, 2, 0)
    w_local.start()
    hid_local.start()
    mask_local.start()
    gate_local.start()
    for i in range(7):
        w_copy(i).start()
    for h in range(2, HEADS_LOCAL):
        for c in local[h]:
            c.wait()

    mask_local.wait()
    for a in range(5):
        for b in range(5):
            blocked = (mask_s[a, b].astype(jnp.float32) - 1.0) * (-NEG)
            far8 = jnp.where(f < 8, blocked[:, 5:6], blocked[:, 0:1])
            for slot, column in ((LEFT, blocked[:, 2:3]), (RIGHT, blocked[:, 3:4]), (FAR8, far8),
                                 (LEFT2, blocked[:, 1:2]), (RIGHT2, blocked[:, 4:5])):
                bias[far_row[slot], a:a + 1, b * BLK:(b + 1) * BLK] = jnp.broadcast_to(column, (1, BLK))
    proj[...] = jnp.zeros_like(proj)
    w_local.wait()
    hid_local.wait()
    gate_local.wait()

    def relay_far(h):
        kv_wait(h, FAR8)
        kv_start(h, 7)

    def relay_near(h):
        @pl.when(f < 8)
        def _():
            kv_wait(h, LEFT)
            kv_start(h, 4)
            kv_wait(h, RIGHT)
            kv_start(h, 5, 6)

        @pl.when(f >= 8)
        def _():
            kv_wait(h, RIGHT)
            kv_start(h, 5)
            kv_wait(h, LEFT)
            kv_start(h, 4, 6)

    def step(h, _):
        @pl.when(both(h < HEADS_LOCAL - 2, jnp.logical_or(h > 0, jnp.logical_not(middle))))
        def _():
            kv_start(h + 2, 1, 2, 0)

        @pl.when(h < HEADS_LOCAL - 3)
        def _():
            relay_far(h + 3)

        m_s[...] = jnp.full_like(m_s, NEG)
        l_s[...] = jnp.zeros_like(l_s)
        acc[...] = jnp.zeros_like(acc)
        attend(h, OWN)
        kv_wait(h, SIB)
        attend(h, SIB)
        attend(h, FAR8)

        @pl.when(h < HEADS_LOCAL - 1)
        def _():
            kv_wait(h + 1, RELAY)
            kv_start(h + 1, 8)
            relay_near(h + 1)

        @pl.when(both(h >= 2, h < DIRECT + 2))
        def _():
            relay_cross(h - 2)

        attend(h, LEFT)
        attend(h, RIGHT)

        @pl.when(h >= 1)
        def _():
            relay_partner(h - 1)

        @pl.when(both(h >= 1, h < DIRECT + 1))
        def _():
            relay_same(h - 1)

        kv_wait(h, FWD)
        attend(h, FWD)

        @pl.when(h == LAST)
        def _():
            for i in SHARED:
                ws_wait(i, 1)
                w_pass(i, 2).start()

        upper = f // 8
        both_sides = both(f >= 4, f < 12)
        pl.when(both_sides)(lambda: kv_wait_any(h, LEFT2 + upper))
        attend(h, LEFT2 + upper, 3 + upper, both_sides)
        kv_wait_any(h, RIGHT2 - upper)
        attend(h, RIGHT2 - upper, 4 - upper, always)
        total = jnp.sum(l_s[...], axis=1, keepdims=True)
        att[g, h] = (acc[...] / total).astype(jnp.bfloat16)
        at_copy(h, 0).start()
        at_copy(h, 1).start()
        at_copy(h, 2).start()

        @pl.when(h >= DIRECT)
        def _():
            at_copy(h, 7).start()

        for after, blocks in enumerate(PASSED):
            @pl.when(h == after)
            def _(blocks=blocks):
                for i in blocks:
                    w_wait(i)
                    w_pass(i, 0).start()
                    if i in SHARED:
                        w_pass(i, 1).start()

        return 0

    relay_far(0)
    kv_start(2, 3)
    relay_far(1)
    kv_start(3, 3)

    @pl.when(middle)
    def _():
        kv_start(2, 1, 2, 0)

    relay_near(0)
    kv_wait(0, RELAY)
    kv_start(0, 8)
    relay_far(2)
    kv_start(4, 3)
    lax.fori_loop(0, HEADS_LOCAL, step, 0)
    relay_partner(LAST)
    for i in range(7):
        ws_wait(i, 0)
        if i in SHARED:
            ws_wait(i, 2)
    relay_cross(3)
    for h in range(LAST):
        project(h)
    project_last()
    gate = gate_s[pl.ds(ts_ref[0], 1), :]
    out_ref[...] = (hid[...].astype(jnp.float32) + gate * proj[...]).astype(out_ref.dtype)

    def drain(h, _):
        for edge in edges:
            if edge[1] is always:
                kv_copy(h, edge).wait_send()
            else:
                @pl.when(edge[1])
                def _(edge=edge):
                    kv_copy(h, edge).wait_send()
        for kind in range(7):
            at_copy(h, kind).wait_send()
        return 0

    lax.fori_loop(0, HEADS_LOCAL, drain, 0)
    for i in range(7):
        w_copy(i).wait_send()
        for kind in range(3 if i in SHARED else 1):
            w_pass(i, kind).wait_send()


def body(hidden_in, queries, keys, values, radial_mask, out_weight, gate_table, timestep):
    any_spec = pl.BlockSpec(memory_space=pl.ANY)
    dma = pltpu.SemaphoreType.DMA
    return pl.pallas_call(
        kernel,
        out_shape=jax.ShapeDtypeStruct((ROWS, ROWS), jnp.bfloat16),
        in_specs=[
            pl.BlockSpec(memory_space=pltpu.SMEM),
            any_spec, any_spec, any_spec, any_spec, any_spec, any_spec, any_spec,
        ],
        out_specs=pl.BlockSpec(memory_space=pltpu.VMEM),
        scratch_shapes=[
            pltpu.VMEM((SLOTS, HEADS_LOCAL, 2, ROWS, HEAD_DIM), jnp.bfloat16),
            pltpu.VMEM((HEADS_LOCAL, ROWS, HEAD_DIM), jnp.bfloat16),
            pltpu.VMEM((GROUPS, HEADS_LOCAL, ROWS, HEAD_DIM), jnp.bfloat16),
            pltpu.VMEM((GROUPS, ROWS, ROWS), jnp.bfloat16),
            pltpu.VMEM((ROWS, ROWS), jnp.bfloat16),
            pltpu.VMEM((5, 5, 1, 6), jnp.int32),
            pltpu.VMEM((50, ROWS), jnp.float32),
            pltpu.VMEM((5, 5, ROWS), jnp.float32),
            pltpu.VMEM((ROWS, HEAD_DIM), jnp.float32),
            pltpu.VMEM((ROWS, HEAD_DIM), jnp.float32),
            pltpu.VMEM((ROWS, HEAD_DIM), jnp.float32),
            pltpu.VMEM((ROWS, ROWS), jnp.float32),
            dma((19,)),
            dma((9, HEADS_LOCAL)), dma((SLOTS, HEADS_LOCAL)),
            dma((7, HEADS_LOCAL)), dma((GROUPS, HEADS_LOCAL)),
            dma((7,)), dma((GROUPS,)), dma((3, 7)), dma((3, GROUPS)),
        ],
        compiler_params=pltpu.CompilerParams(
            collective_id=0, has_side_effects=True, vmem_limit_bytes=60 * 1024 * 1024),
        cost_estimate=pl.CostEstimate(
            flops=14_000_000_000, bytes_accessed=12_000_000, transcendentals=16_000_000),
    )(timestep, radial_mask.transpose(2, 3, 0, 1), gate_table, hidden_in, queries, keys, values, out_weight)


def solution(mesh):
    in_specs = (
        P("frame", "head"), P("frame", "head"), P("frame", "head"), P("frame", "head"),
        P("frame", None, None, None), P("head", None), P(None, "head"), P(),
    )
    return jax.shard_map(
        body, mesh=mesh, in_specs=in_specs, out_specs=P("frame", "head"), check_vma=False)
```
